128 devices in a mesh: ctx: 32 (over x, z_lo, y), head: 4 (over z_hi, core).
Axes of the slice: x: 4, y: 4, z: 4 (z_hi: 2, z_lo: 2; z = z_hi * 2 + z_lo), core: 2. Of those that a mesh axis runs over, the one named last changes fastest.
Arguments:
- queries: bfloat16 [1024, 128, 128], P('ctx', 'head'), may hold values from -60 to 60
- cache_keys: bfloat16 [40960, 8, 128], P('ctx', 'head'), may hold values from -9 to 9
- cache_values: bfloat16 [40960, 8, 128], P('ctx', 'head'), may hold values from -6 to 6
- new_keys: bfloat16 [1024, 8, 128], P('ctx', 'head'), may hold values from -6 to 6
- new_values: bfloat16 [1024, 8, 128], P('ctx', 'head'), may hold values from -6 to 6
- lengths: int32 [32], P('ctx'), may hold values from 2 to 1280
- span_offset: int32 [], replicated, may hold values from 0 to 1023
Outputs:
- attended: bfloat16 [1024, 128, 128], P(('ctx', 'head'))
The draws below stay inside these ranges and needn't reach their ends.
All inputs are finite; a program needn't handle non-finite values.
Results may differ from the reference program's by a relative error of at most 0.0056.
Values may be sent and summed in bfloat16 or wider, within the bound.
No kernel may reach another device: no remote copies, remote signals or barrier semaphores. Data moves between devices by JAX's collectives and lax.ppermute only.
A program may use at most 128 MiB of HBM per device.

```python
import jax
import jax.numpy as jnp
from jax import lax

HEADS = 128
KVH = 8
HD = 128
C_DEV = 1280
Q_DEV = 32
SHARDS = 32
CACHE = 40960
NEW = 1024
N_CTX = 32


def shared_base(key):
    return jnp.clip(jax.random.normal(key, (CACHE, KVH, HD), jnp.float32), -4.5, 4.5)


def draw_cache_keys(key, part):
    base = shared_base(key)
    cache_draw = base
    return cache_draw.astype(jnp.bfloat16)


def draw_queries(key, part):
    key = jax.random.fold_in(key, 5)
    values = jnp.clip(jax.random.normal(key, (NEW, HEADS, HD), jnp.float32), -4.5, 4.5)
    return values.astype(jnp.bfloat16)


def plant(entries, own_key, least, high):
    index_at = [jax.random.randint(jax.random.fold_in(own_key, axis), (), 0, length) for axis, length in enumerate(entries.shape)]
    widest = entries.shape.index(max(entries.shape))
    next_to = index_at[:widest] + [(index_at[widest] + 1) % entries.shape[widest]] + index_at[widest + 1:]
    return entries.at[tuple(index_at)].set(least).at[tuple(next_to)].set(high)


def shard_levels(rng, dims, cuts, low, largest):
    def one(position, parts):
        draws = jax.random.uniform(jax.random.fold_in(jax.random.fold_in(rng, 6), position), (parts,), jnp.float32, low / len(cuts), largest / len(cuts))
        return jnp.repeat(jnp.exp(draws), dims[position] // parts).reshape((-1,) + (1,) * (len(dims) - position - 1))

    factor_of = one(*cuts[0])
    for cut in cuts[1:]:
        factor_of = factor_of * one(*cut)
    return factor_of


def noise(stream_key, dims, scale, reach, split=(), kind=jnp.bfloat16):
    level = shard_levels(stream_key, dims, split, -0.22, 0.18) if split else 1.0
    values = jax.random.normal(stream_key, dims, jnp.float32) * scale * level
    return jnp.minimum(jnp.maximum(values, -reach), reach).astype(kind)


def setup_inputs(seed: int = 0) -> dict:
    streams_of = jax.random.split(jax.random.key(seed), 8)
    return {
        "queries": draw_queries(jax.random.fold_in(streams_of[7], 71), 0),
        "cache_keys": draw_cache_keys(jax.random.fold_in(streams_of[7], 71), 0),
        "cache_values": noise(streams_of[2], (CACHE, KVH, HD), 1.0, 6.0, ((0, 32), (1, 4))),
        "new_keys": noise(streams_of[3], (NEW, KVH, HD), 1.0, 6.0, ((0, 32), (1, 4))),
        "new_values": noise(streams_of[4], (NEW, KVH, HD), 1.0, 6.0, ((0, 32), (1, 4))),
        "lengths": plant(jax.random.randint(streams_of[5], (SHARDS,), 2, C_DEV + 1), jax.random.fold_in(streams_of[5], 1), 2, C_DEV).astype(jnp.int32),
        "span_offset": jax.random.randint(streams_of[6], (), 0, NEW).astype(jnp.int32),
    }


def block_partial(queries, key_rows, value_rows, cache_length, query_start, key_start, offset):
    query_rows, head_count, head_width = queries.shape
    kv_heads = key_rows.shape[1]
    group_size = head_count // kv_heads
    total_keys = key_rows.shape[0]
    cache_rows = total_keys - query_rows
    grouped = queries.reshape(query_rows, kv_heads, group_size, head_width).astype(jnp.float32)
    scores = jnp.einsum("rkgd,ckd->rkgc", grouped, key_rows.astype(jnp.float32)) * (head_width ** -0.5)
    key_slots = lax.broadcasted_iota(jnp.int32, (query_rows, total_keys), 1)
    row_limit = query_start + offset + lax.broadcasted_iota(jnp.int32, (query_rows, total_keys), 0)
    visible = jnp.where(key_slots < cache_rows, key_slots < cache_length, key_start + key_slots - cache_rows <= row_limit)
    visible = visible[:, None, None, :]
    masked = jnp.where(visible, scores, jnp.float32(-1e30))
    maxima = jnp.max(masked, axis=-1)
    probabilities = jnp.where(visible, jnp.exp(masked - maxima[..., None]), jnp.float32(0.0))
    totals = jnp.sum(probabilities, axis=-1)
    low = probabilities.astype(jnp.bfloat16).astype(jnp.float32)
    weighted = jnp.einsum("rkgc,ckd->rkgd", low, value_rows.astype(jnp.float32))
    partial_out = (weighted / totals[..., None]).astype(jnp.bfloat16)
    return (partial_out.reshape(query_rows, head_count, head_width),
            maxima.reshape(query_rows, head_count), totals.reshape(query_rows, head_count))


def reference(queries, cache_keys, cache_values, new_keys, new_values, lengths, span_offset):
    blocks = queries.reshape(N_CTX, Q_DEV, HEADS, HD)
    block_ids = jnp.arange(N_CTX, dtype=jnp.int32)

    def shard(state_now, shard_index):
        running_max, running_sum, running_out = state_now
        shard_keys = jnp.concatenate([
            lax.dynamic_slice_in_dim(cache_keys, (shard_index * C_DEV).astype(jnp.int32), C_DEV, 0),
            lax.dynamic_slice_in_dim(new_keys, (shard_index * Q_DEV).astype(jnp.int32), Q_DEV, 0)], 0)
        shard_values = jnp.concatenate([
            lax.dynamic_slice_in_dim(cache_values, (shard_index * C_DEV).astype(jnp.int32), C_DEV, 0),
            lax.dynamic_slice_in_dim(new_values, (shard_index * Q_DEV).astype(jnp.int32), Q_DEV, 0)], 0)

        def one_block(block_pair):
            query_block, block_index = block_pair
            return block_partial(query_block, shard_keys, shard_values, lengths[shard_index],
                                 block_index * Q_DEV, shard_index * Q_DEV, span_offset)

        partials, maxima, totals = lax.map(one_block, (blocks, block_ids))
        partials = partials.reshape(NEW, HEADS, HD).astype(jnp.float32)
        maxima = maxima.reshape(NEW, HEADS)
        totals = totals.reshape(NEW, HEADS)
        new_max = jnp.maximum(running_max, maxima)
        scale_old = jnp.exp(running_max - new_max)
        scale_new = totals * jnp.exp(maxima - new_max)
        running_sum = running_sum * scale_old + scale_new
        running_out = running_out * scale_old[..., None] + scale_new[..., None] * partials
        return (new_max, running_sum, running_out), None

    initial = (jnp.full((NEW, HEADS), -1e30, jnp.float32), jnp.zeros((NEW, HEADS), jnp.float32),
               jnp.zeros((NEW, HEADS, HD), jnp.float32))
    final, _ = lax.scan(shard, initial, block_ids)
    return (final[2] / final[1][..., None]).astype(jnp.bfloat16)
```

```python
import functools
import math

import jax
import jax.numpy as jnp
from jax import lax
from jax.experimental import pallas as pl
from jax.experimental.pallas import tpu as pltpu
from jax.sharding import Mesh, PartitionSpec as P

F32 = jnp.float32
BF16 = jnp.bfloat16
SCALE = math.log2(math.e) / math.sqrt(128)
HIDDEN = -1e30
SUM_LIMIT = 1e30
SLOTS = 1280
SPAN = 32
KEYS = SLOTS + SPAN
GROUP = 16
ROWS = SPAN * GROUP
BLOCKS = 8
SUB = 256
NOTE = 144
HALVES = 2


def times_transposed(a, b):
    return lax.dot_general(a, b, (((1,), (1,)), ((), ())), preferred_element_type=F32)


def times(a, b):
    return jnp.dot(a, b, preferred_element_type=F32)


def attend_kernel(
    lengths, key_start, query_start, place, *refs, head
):
    q_in = refs[:BLOCKS]
    own, left, right, far_k, far_v = refs[BLOCKS : BLOCKS + 5]
    out, q_ref, kv_ref, acc, top, fresh, sems = refs[BLOCKS + 5 :]
    copies = []
    for b in range(BLOCKS):
        copies.append((q_in[b].at[:, head * GROUP : (head + 1) * GROUP, :], q_ref.at[b]))
    for s, source in enumerate((own, left, right)):
        copies.append((source, kv_ref.at[s]))
    copies.append((far_k, kv_ref.at[3, 0]))
    copies.append((far_v, kv_ref.at[3, 1]))
    copies = [pltpu.make_async_copy(a, b, sems.at[n]) for n, (a, b) in enumerate(copies)]
    for copy in copies:
        copy.start()
    for copy in copies:
        copy.wait()

    lane = lax.broadcasted_iota(jnp.int32, (1, 128), 1)
    slot = lax.broadcasted_iota(jnp.int32, (128, 1), 0)
    begins = [jnp.int32(0)]
    for s in range(4):
        begins.append(begins[-1] + (lengths[s] + 127) // 128)
    count = begins[4]

    def half(index):
        shard, begin, length = jnp.int32(0), jnp.int32(0), lengths[0]
        for s in range(1, 4):
            later = index >= begins[s]
            shard = jnp.where(later, s, shard)
            begin = jnp.where(later, begins[s], begin)
            length = jnp.where(later, lengths[s], length)
        row = (index - begin) * 128
        exists = index < count
        filled = jnp.where(exists, length - row, 0)
        row = jnp.where(exists, row, 0)
        return shard, pl.multiple_of(row, 128), filled

    for s in range(4):
        for part in range(2):
            fresh[part, s * SPAN : (s + 1) * SPAN] = kv_ref[s, part, SLOTS:KEYS]
    position = jnp.zeros((1, 128), jnp.int32)
    for s in range(4):
        position = jnp.where(lane // SPAN == s, key_start[s] + lane - s * SPAN, position)

    def queries_of(r):
        first = (r % ROWS) // GROUP
        return q_ref[r // ROWS, first : first + SUB // GROUP].reshape(SUB, 128)

    def limit_of(block, first):
        token = lax.broadcasted_iota(jnp.int32, (SUB, 128), 0) // GROUP
        return token + (query_start[block] + first)

    ones = jnp.ones((128, 128), BF16)
    k_first = jnp.concatenate([fresh[0], kv_ref[0, 0, 0:128]], 0)
    v_first = jnp.concatenate([fresh[1], kv_ref[0, 1, 0:128]], 0)
    v_first = jnp.concatenate([v_first, jnp.concatenate([ones, ones], 0)], 1)
    for r in range(0, BLOCKS * ROWS, SUB):
        scores = times_transposed(queries_of(r), k_first)
        limit = limit_of(r // ROWS, (r % ROWS) // GROUP)
        s0 = jnp.where(position <= limit, scores[:, :128], HIDDEN)
        s1 = jnp.where(lane < lengths[0], scores[:, 128:], HIDDEN)
        largest = jnp.max(jnp.maximum(s0, s1), axis=1, keepdims=True)
        base = jnp.broadcast_to(largest * SCALE, (SUB, 128))
        top[r : r + SUB] = base
        p0 = jnp.exp2(s0 * SCALE - base).astype(BF16)
        p1 = jnp.exp2(s1 * SCALE - base).astype(BF16)
        acc[r : r + SUB] = times(jnp.concatenate([p0, p1], 1), v_first)

    def step(number, carry):
        parts = [half(HALVES * number + g + 1) for g in range(HALVES)]
        k = jnp.concatenate([kv_ref[s, 0, pl.ds(row, 128)] for s, row, _ in parts], 0)
        v = jnp.concatenate(
            [
                jnp.concatenate(
                    [
                        jnp.where(slot < filled, kv_ref[s, 1, pl.ds(row, 128)], 0),
                        jnp.where(slot < filled, ones, 0),
                    ],
                    1,
                )
                for s, row, filled in parts
            ],
            0,
        )
        for r in range(0, BLOCKS * ROWS, SUB):
            scores = times_transposed(queries_of(r), k)
            base = top[r : r + SUB]
            probs = [
                jnp.exp2(scores[:, g * 128 : (g + 1) * 128] * SCALE - base).astype(BF16)
                for g in range(HALVES)
            ]
            acc[r : r + SUB] += times(jnp.concatenate(probs, 1), v)
        return carry

    lax.fori_loop(0, (count - 1 + HALVES - 1) // HALVES, step, 0)

    wrong = jnp.zeros((8, 128), F32)
    for r in range(0, BLOCKS * ROWS, 8):
        wrong = jnp.maximum(wrong, jnp.where(acc[r : r + 8, 128:] < SUM_LIMIT, 0.0, 1.0))

    @pl.when(jnp.max(wrong) > 0.5)
    def _():
        def redo(tile, carry):
            block, first = tile // 2, (tile % 2) * (SUB // GROUP)
            rows = pl.ds(pl.multiple_of(tile * SUB, SUB), SUB)
            q = q_ref[block, pl.ds(first, SUB // GROUP)].reshape(SUB, 128)

            def absorb(scores, v, state):
                old, total = state
                new = jnp.maximum(old, jnp.max(scores, axis=1, keepdims=True) * SCALE)
                shrink = jnp.exp2(old - new)
                p = jnp.exp2(scores * SCALE - new)
                total = total * shrink + jnp.sum(p, axis=1, keepdims=True)
                acc[rows, 0:128] = acc[rows, 0:128] * shrink + times(p.astype(BF16), v)
                return new, total

            acc[rows] = jnp.zeros((SUB, 256), F32)
            state = (jnp.full((SUB, 1), HIDDEN, F32), jnp.zeros((SUB, 1), F32))

            def more(index, state):
                s, row, filled = half(index)
                scores = times_transposed(q, kv_ref[s, 0, pl.ds(row, 128)])
                scores = jnp.where(lane < filled, scores, HIDDEN)
                return absorb(scores, kv_ref[s, 1, pl.ds(row, 128)], state)

            state = lax.fori_loop(0, count, more, state)
            scores = times_transposed(q, fresh[0])
            scores = jnp.where(position <= limit_of(block, first), scores, HIDDEN)
            base, total = absorb(scores, fresh[1], state)
            top[rows] = jnp.broadcast_to(base, (SUB, 128))
            acc[rows, 128:256] = jnp.broadcast_to(total, (SUB, 128))
            return carry

        lax.fori_loop(0, BLOCKS * ROWS // SUB, redo, 0)

    diagonal = lax.broadcasted_iota(jnp.int32, (128, 128), 0) == lane
    for b in range(BLOCKS):
        for quarter in range(4):
            r = b * ROWS + quarter * 128
            total = acc[r : r + 128, 128:]
            out[place[b], quarter, 0:128] = (acc[r : r + 128, 0:128] / total).astype(BF16)
            lse = top[r : r + 128] + jnp.log2(total)
            lse = jnp.sum(jnp.where(diagonal, lse, 0.0), axis=0, keepdims=True)
            high = lse.astype(BF16).astype(F32)
            middle = (lse - high).astype(BF16).astype(F32)
            low = lse - high - middle
            row = lax.broadcasted_iota(jnp.int32, (16, 128), 0)
            note = jnp.where(row == 0, high, jnp.where(row == 1, middle, jnp.where(row == 2, low, 0.0)))
            out[place[b], quarter, 128:NOTE] = note.astype(BF16)


def attend(scalars, queries, kv, head):
    return pl.pallas_call(
        functools.partial(attend_kernel, head=head),
        out_shape=jax.ShapeDtypeStruct((BLOCKS, 4, NOTE, 128), BF16),
        in_specs=[pl.BlockSpec(memory_space=pltpu.SMEM)] * 4
        + [pl.BlockSpec(memory_space=pl.ANY)] * (BLOCKS + 5),
        out_specs=pl.BlockSpec(memory_space=pltpu.VMEM),
        scratch_shapes=[
            pltpu.VMEM((BLOCKS, SPAN, GROUP, 128), BF16),
            pltpu.VMEM((4, 2, KEYS, 128), BF16),
            pltpu.VMEM((BLOCKS * ROWS, 256), F32),
            pltpu.VMEM((BLOCKS * ROWS, 128), F32),
            pltpu.VMEM((2, 128, 128), BF16),
            pltpu.SemaphoreType.DMA((BLOCKS + 5,)),
        ],
        compiler_params=pltpu.CompilerParams(vmem_limit_bytes=40 << 20),
        cost_estimate=pl.CostEstimate(
            flops=2 * 2 * BLOCKS * ROWS * 4 * KEYS * 256,
            bytes_accessed=8 << 20,
            transcendentals=0,
        ),
        name="attend",
    )(*scalars, *queries, *kv)


def merge_kernel(first, second, out):
    eye = lax.broadcasted_iota(jnp.int32, (128, 128), 0) == lax.broadcasted_iota(jnp.int32, (128, 128), 1)
    for source in range(4):
        for head, ref in enumerate((first, second)):
            lse = []
            for b in range(BLOCKS):
                note = ref[b * 4 + source, 128:NOTE].astype(F32)
                lse.append(note[0:1] + note[1:2] + note[2:3])
            largest = functools.reduce(jnp.maximum, lse)
            weights = [jnp.exp2(x - largest) for x in lse]
            total = functools.reduce(jnp.add, weights)
            left, right = [], []
            for b in range(BLOCKS):
                weight = jnp.broadcast_to(weights[b] / total, (128, 128))
                high = weight.astype(BF16)
                low = (weight - high.astype(F32)).astype(BF16)
                left += [jnp.where(eye, high, 0), jnp.where(eye, low, 0)]
                partial = ref[b * 4 + source, 0:128]
                right += [partial, partial]
            merged = times(jnp.concatenate(left, 1), jnp.concatenate(right, 0))
            begin = source * 32 + head * GROUP
            out[:, begin : begin + GROUP] = merged.astype(BF16).reshape(8, GROUP, 128)


def merge(first, second):
    return pl.pallas_call(
        merge_kernel,
        out_shape=jax.ShapeDtypeStruct((8, 128, 128), BF16),
        in_specs=[pl.BlockSpec(memory_space=pltpu.VMEM)] * 2,
        out_specs=pl.BlockSpec(memory_space=pltpu.VMEM),
        compiler_params=pltpu.CompilerParams(vmem_limit_bytes=32 << 20),
        name="merge",
    )(first, second)


def moved(block, axis, distance):
    size = lax.axis_size(axis)
    return lax.ppermute(block, axis, [(i, (i + distance) % size) for i in range(size)])


def per_device(queries, cache_keys, cache_values, new_keys, new_values, lengths, span_offset):
    x, z, y = lax.axis_index("x"), lax.axis_index("z"), lax.axis_index("y")

    def packed(head):
        k = jnp.concatenate([cache_keys[:, head], new_keys[:, head]], 0)
        v = jnp.concatenate([cache_values[:, head], new_values[:, head]], 0)
        return jnp.stack([k, v])

    def gathered(own):
        left, right = moved(own, "y", 1), moved(own, "y", -1)
        return own, left, right, moved(left[0], "y", 1), moved(right[1], "y", -1)

    all_lengths = lax.all_gather(lengths[0], "y")
    beside = moved(queries, "z", 1)
    blocks, homes = [], []
    for dz, block in enumerate((queries, beside)):
        for dx in (0, 1, -1, 2):
            blocks.append(moved(block, "x", -dx) if dx else block)
            homes.append(((x + dx) % 4, (z + dz) % 2))
    place = jnp.stack([hx * 2 + hz for hx, hz in homes]).astype(jnp.int32)
    query_start = jnp.stack([(hx * 8 + hz * 4 + y) * SPAN for hx, hz in homes]).astype(jnp.int32) + span_offset
    shards = jnp.stack([y, (y - 1) % 4, (y + 1) % 4, (y + 2) % 4]).astype(jnp.int32)
    key_start = (x * 8 + z * 4 + shards) * SPAN
    scalars = (all_lengths[shards], key_start, query_start, place)

    kv = [gathered(packed(head)) for head in range(2)]
    partials = []
    for head in range(2):
        partial = attend(scalars, blocks, kv[head], head)
        partials.append(
            lax.all_to_all(
                partial.reshape(BLOCKS * 4, NOTE, 128), ("x", "z", "head"), 0, 0, tiled=True
            )
        )
    return merge(*partials)


def solution(mesh):
    inner = Mesh(mesh.devices.reshape(4, 2, 4, 4), ("x", "z", "y", "head"))
    context = ("x", "z", "y")
    return jax.shard_map(
        per_device,
        mesh=inner,
        in_specs=(
            P(context, "head", None),
            P(context, "head", None),
            P(context, "head", None),
            P(context, "head", None),
            P(context, "head", None),
            P(context),
            P(),
        ),
        out_specs=P((*context, "head"), None, None),
        check_vma=False,
    )
```

```python
import functools
import math

import jax
import jax.numpy as jnp
from jax import lax
from jax.experimental import pallas as pl
from jax.experimental.pallas import tpu as pltpu
from jax.sharding import Mesh, PartitionSpec as P

F32 = jnp.float32
BF16 = jnp.bfloat16
SCALE = math.log2(math.e) / math.sqrt(128)
HIDDEN = -1e30
SUM_LIMIT = 1e30
SLOTS = 1280
SPAN = 32
KEYS = SLOTS + SPAN
PACKED = KEYS + 16
GROUP = 16
ROWS = SPAN * GROUP
BLOCKS = 8
SUB = 256
NOTE = 144
HALVES = 8


def times_transposed(a, b):
    return lax.dot_general(a, b, (((1,), (1,)), ((), ())), preferred_element_type=F32)


def times(a, b):
    return jnp.dot(a, b, preferred_element_type=F32)


def attend_kernel(
    key_start, query_start, place, *refs, head
):
    q_in = refs[:4]
    shards = refs[4:8]
    out, q_ref, kv_ref, acc, top, fresh, sums, sems = refs[8:]
    copies = []
    for b in range(BLOCKS):
        copies.append((q_in[b // 2].at[b % 2, :, head * GROUP : (head + 1) * GROUP, :], q_ref.at[b]))
    for s, source in enumerate(shards):
        copies.append((source, kv_ref.at[s]))
    copies = [pltpu.make_async_copy(a, b, sems.at[n]) for n, (a, b) in enumerate(copies)]
    for copy in copies:
        copy.start()
    for copy in copies:
        copy.wait()

    lane = lax.broadcasted_iota(jnp.int32, (1, 128), 1)
    slot = lax.broadcasted_iota(jnp.int32, (128, 1), 0)
    lengths = []
    for s in range(4):
        digits = kv_ref[s, 0, KEYS:PACKED].astype(F32)
        lengths.append((jnp.max(digits[0:1]) * 16.0 + jnp.max(digits[1:2])).astype(jnp.int32))
    begins = [jnp.int32(0)]
    for s in range(4):
        begins.append(begins[-1] + (lengths[s] + 127) // 128)
    count = begins[4]

    def half(index):
        shard, begin, length = jnp.int32(0), jnp.int32(0), lengths[0]
        for s in range(1, 4):
            later = index >= begins[s]
            shard = jnp.where(later, s, shard)
            begin = jnp.where(later, begins[s], begin)
            length = jnp.where(later, lengths[s], length)
        row = (index - begin) * 128
        exists = index < count
        filled = jnp.where(exists, length - row, 0)
        row = jnp.where(exists, row, 0)
        return shard, pl.multiple_of(row, 128), filled

    for s in range(4):
        for part in range(2):
            fresh[part, s * SPAN : (s + 1) * SPAN] = kv_ref[s, part, SLOTS:KEYS]
    position = jnp.zeros((1, 128), jnp.int32)
    for s in range(4):
        position = jnp.where(lane // SPAN == s, key_start[s] + lane - s * SPAN, position)

    def queries_of(r):
        first = (r % ROWS) // GROUP
        return q_ref[r // ROWS, first : first + SUB // GROUP].reshape(SUB, 128)

    def limit_of(block, first):
        token = lax.broadcasted_iota(jnp.int32, (SUB, 128), 0) // GROUP
        return token + (query_start[block] + first)

    ones = jnp.ones((128, 128), BF16)
    k_first = jnp.concatenate([fresh[0], kv_ref[0, 0, 0:128]], 0)
    v_first = jnp.concatenate([fresh[1], kv_ref[0, 1, 0:128]], 0)
    v_first = jnp.concatenate([v_first, jnp.concatenate([ones, ones], 0)], 1)
    for r in range(0, BLOCKS * ROWS, SUB):
        scores = times_transposed(queries_of(r), k_first)
        limit = limit_of(r // ROWS, (r % ROWS) // GROUP)
        s0 = jnp.where(position <= limit, scores[:, :128], HIDDEN)
        s1 = jnp.where(lane < lengths[0], scores[:, 128:], HIDDEN)
        largest = jnp.max(jnp.maximum(s0, s1), axis=1, keepdims=True)
        base = jnp.broadcast_to(largest * SCALE, (SUB, 128))
        top[r : r + SUB] = base
        p0 = jnp.exp2(s0 * SCALE - base).astype(BF16)
        p1 = jnp.exp2(s1 * SCALE - base).astype(BF16)
        acc[r : r + SUB] = times(jnp.concatenate([p0, p1], 1), v_first)

    def step(first, halves):
        parts = [half(first + g) for g in range(halves)]
        k = jnp.concatenate([kv_ref[s, 0, pl.ds(row, 128)] for s, row, _ in parts], 0)
        v = jnp.concatenate(
            [
                jnp.concatenate(
                    [
                        jnp.where(slot < filled, kv_ref[s, 1, pl.ds(row, 128)], 0),
                        jnp.where(slot < filled, ones, 0),
                    ],
                    1,
                )
                for s, row, filled in parts
            ],
            0,
        )
        for r in range(0, BLOCKS * ROWS, SUB):
            scores = times_transposed(queries_of(r), k)
            base = top[r : r + SUB]
            probs = [
                jnp.exp2(scores[:, g * 128 : (g + 1) * 128] * SCALE - base).astype(BF16)
                for g in range(halves)
            ]
            acc[r : r + SUB] += times(jnp.concatenate(probs, 1), v)

    def full_step(number, carry):
        step(HALVES * number + 1, HALVES)
        return carry

    steps = count // HALVES
    lax.fori_loop(0, steps, full_step, 0)
    begun = steps * HALVES + 1
    pairs = (jnp.maximum(count - begun, 0) + 1) // 2

    @pl.when(pairs >= 2)
    def _():
        step(begun, 4)

    @pl.when(pairs % 2 == 1)
    def _():
        step(begun + pairs // 2 * 4, 2)

    diagonal = lax.broadcasted_iota(jnp.int32, (128, 128), 0) == lane

    def in_rows(array, begin):
        rows = []
        for r in range(0, BLOCKS * ROWS, 128):
            square = jnp.where(diagonal, array[r : r + 128, begin : begin + 128], 0.0)
            rows.append(jnp.sum(square, axis=0, keepdims=True))
        return jnp.concatenate(rows, 0)

    sums[...] = in_rows(acc, 128)
    wrong = jnp.where(sums[...] < SUM_LIMIT, 0.0, 1.0)

    @pl.when(jnp.max(wrong) > 0.5)
    def _():
        def redo(tile, carry):
            block, first = tile // 2, (tile % 2) * (SUB // GROUP)
            rows = pl.ds(pl.multiple_of(tile * SUB, SUB), SUB)
            q = q_ref[block, pl.ds(first, SUB // GROUP)].reshape(SUB, 128)

            def absorb(scores, v, state):
                old, total = state
                new = jnp.maximum(old, jnp.max(scores, axis=1, keepdims=True) * SCALE)
                shrink = jnp.exp2(old - new)
                p = jnp.exp2(scores * SCALE - new)
                total = total * shrink + jnp.sum(p, axis=1, keepdims=True)
                acc[rows, 0:128] = acc[rows, 0:128] * shrink + times(p.astype(BF16), v)
                return new, total

            acc[rows] = jnp.zeros((SUB, 256), F32)
            state = (jnp.full((SUB, 1), HIDDEN, F32), jnp.zeros((SUB, 1), F32))

            def more(index, state):
                s, row, filled = half(index)
                scores = times_transposed(q, kv_ref[s, 0, pl.ds(row, 128)])
                scores = jnp.where(lane < filled, scores, HIDDEN)
                return absorb(scores, kv_ref[s, 1, pl.ds(row, 128)], state)

            state = lax.fori_loop(0, count, more, state)
            scores = times_transposed(q, fresh[0])
            scores = jnp.where(position <= limit_of(block, first), scores, HIDDEN)
            base, total = absorb(scores, fresh[1], state)
            top[rows] = jnp.broadcast_to(base, (SUB, 128))
            acc[rows, 128:256] = jnp.broadcast_to(total, (SUB, 128))
            return carry

        lax.fori_loop(0, BLOCKS * ROWS // SUB, redo, 0)
        sums[...] = in_rows(acc, 128)

    notes = []
    for value in (in_rows(top, 0), sums[...]):
        high = value.astype(BF16)
        rest = value - high.astype(F32)
        middle = rest.astype(BF16)
        notes += [high, middle, (rest - middle.astype(F32)).astype(BF16)]
    blank = jnp.zeros((NOTE - 128 - 6, 128), BF16)
    for b in range(BLOCKS):
        for quarter in range(4):
            n = b * 4 + quarter
            out[place[b], quarter, 0:128] = acc[n * 128 : n * 128 + 128, 0:128].astype(BF16)
            rows = [note[n : n + 1] for note in notes]
            out[place[b], quarter, 128:NOTE] = jnp.concatenate([*rows, blank], 0)


def attend(scalars, queries, kv, head):
    return pl.pallas_call(
        functools.partial(attend_kernel, head=head),
        out_shape=jax.ShapeDtypeStruct((BLOCKS, 4, NOTE, 128), BF16),
        in_specs=[pl.BlockSpec(memory_space=pltpu.SMEM)] * 3
        + [pl.BlockSpec(memory_space=pltpu.HBM)] * 8,
        out_specs=pl.BlockSpec(memory_space=pltpu.VMEM),
        scratch_shapes=[
            pltpu.VMEM((BLOCKS, SPAN, GROUP, 128), BF16),
            pltpu.VMEM((4, 2, PACKED, 128), BF16),
            pltpu.VMEM((BLOCKS * ROWS, 256), F32),
            pltpu.VMEM((BLOCKS * ROWS, 128), F32),
            pltpu.VMEM((2, 128, 128), BF16),
            pltpu.VMEM((BLOCKS * 4, 128), F32),
            pltpu.SemaphoreType.DMA((BLOCKS + 4,)),
        ],
        compiler_params=pltpu.CompilerParams(vmem_limit_bytes=62 << 20),
        cost_estimate=pl.CostEstimate(
            flops=2 * 2 * BLOCKS * ROWS * 4 * KEYS * 256,
            bytes_accessed=8 << 20,
            transcendentals=0,
        ),
        name="attend",
    )(*scalars, *queries, *kv)


def merge_kernel(first, second, out):
    eye = lax.broadcasted_iota(jnp.int32, (128, 128), 0) == lax.broadcasted_iota(jnp.int32, (128, 128), 1)
    for source in range(4):
        for head, ref in enumerate((first, second)):
            tops, sums = [], []
            for b in range(BLOCKS):
                note = ref[b * 4 + source, 128:NOTE].astype(F32)
                tops.append(note[0:1] + note[1:2] + note[2:3])
                sums.append(note[3:4] + note[4:5] + note[5:6])
            largest = functools.reduce(jnp.maximum, tops)
            weights = [jnp.exp2(t - largest) for t in tops]
            total = functools.reduce(jnp.add, [w * s for w, s in zip(weights, sums)])
            left, right = [], []
            for b in range(BLOCKS):
                weight = jnp.broadcast_to(weights[b] / total, (128, 128))
                high = weight.astype(BF16)
                low = (weight - high.astype(F32)).astype(BF16)
                left += [jnp.where(eye, high, 0), jnp.where(eye, low, 0)]
                partial = ref[b * 4 + source, 0:128]
                right += [partial, partial]
            merged = times(jnp.concatenate(left, 1), jnp.concatenate(right, 0))
            begin = source * 32 + head * GROUP
            out[:, begin : begin + GROUP] = merged.astype(BF16).reshape(8, GROUP, 128)


def merge(first, second):
    return pl.pallas_call(
        merge_kernel,
        out_shape=jax.ShapeDtypeStruct((8, 128, 128), BF16),
        in_specs=[pl.BlockSpec(memory_space=pltpu.VMEM)] * 2,
        out_specs=pl.BlockSpec(memory_space=pltpu.VMEM),
        compiler_params=pltpu.CompilerParams(vmem_limit_bytes=32 << 20),
        name="merge",
    )(first, second)


def moved(block, axis, distance):
    size = lax.axis_size(axis)
    return lax.ppermute(block, axis, [(i, (i + distance) % size) for i in range(size)])


def per_device(queries, cache_keys, cache_values, new_keys, new_values, lengths, span_offset):
    x, z, y = lax.axis_index("x"), lax.axis_index("z"), lax.axis_index("y")

    digit = lax.broadcasted_iota(jnp.int32, (16, 128), 0)
    length = lengths[0]
    tail = jnp.where(digit == 0, length // 16, jnp.where(digit == 1, length % 16, 0)).astype(BF16)

    def packed(head):
        k = jnp.concatenate([cache_keys[:, head], new_keys[:, head], tail], 0)
        v = jnp.concatenate([cache_values[:, head], new_values[:, head], tail], 0)
        return jnp.stack([k, v])

    beside = moved(queries, "z", 1)
    queries, beside, cache_keys, cache_values = lax.optimization_barrier(
        (queries, beside, cache_keys, cache_values)
    )
    own = packed(0)
    left, right, far = (moved(own, "y", distance) for distance in (1, -1, 2))
    both = jnp.stack([queries, beside])
    after, before = moved(both, "x", -1), moved(both, "x", 1)
    both_too, after, before = lax.optimization_barrier((both, after, before))
    blocks = (both, after, before, moved(both_too, "x", 2))
    left, right, far, late_own = lax.optimization_barrier((left, right, far, packed(1)))
    early = (own, left, right, far)
    late = (late_own, *(moved(late_own, "y", distance) for distance in (1, -1, 2)))
    kv = (early, late)
    homes = [((x + dx) % 4, (z + dz) % 2) for dx in (0, 1, -1, 2) for dz in (0, 1)]
    place = jnp.stack([hx * 2 + hz for hx, hz in homes]).astype(jnp.int32)
    query_start = jnp.stack([(hx * 8 + hz * 4 + y) * SPAN for hx, hz in homes]).astype(jnp.int32) + span_offset
    shards = jnp.stack([y, (y - 1) % 4, (y + 1) % 4, (y + 2) % 4]).astype(jnp.int32)
    key_start = (x * 8 + z * 4 + shards) * SPAN
    scalars = (key_start, query_start, place)

    partials = []
    for head in range(2):
        partial = attend(scalars, blocks, kv[head], head)
        partials.append(
            lax.all_to_all(
                partial.reshape(BLOCKS * 4, NOTE, 128), ("x", "z", "head"), 0, 0, tiled=True
            )
        )
    return merge(*partials)


def solution(mesh):
    inner = Mesh(mesh.devices.reshape(4, 2, 4, 4), ("x", "z", "y", "head"))
    context = ("x", "z", "y")
    return jax.shard_map(
        per_device,
        mesh=inner,
        in_specs=(
            P(context, "head", None),
            P(context, "head", None),
            P(context, "head", None),
            P(context, "head", None),
            P(context, "head", None),
            P(context),
            P(),
        ),
        out_specs=P((*context, "head"), None, None),
        check_vma=False,
    )
```

```python
import functools
import math

import jax
import jax.numpy as jnp
from jax import lax
from jax.experimental import pallas as pl
from jax.experimental.pallas import tpu as pltpu
from jax.sharding import Mesh, PartitionSpec as P

F32 = jnp.float32
BF16 = jnp.bfloat16
SCALE = math.log2(math.e) / math.sqrt(128)
HIDDEN = -1e30
SUM_LIMIT = 1e30
SLOTS = 1280
SPAN = 32
KEYS = SLOTS + SPAN
PACKED = KEYS + 16
GROUP = 16
ROWS = SPAN * GROUP
BLOCKS = 8
SUB = 256
NOTE = 144
HALVES = 8


def times_transposed(a, b):
    return lax.dot_general(a, b, (((1,), (1,)), ((), ())), preferred_element_type=F32)


def times(a, b):
    return jnp.dot(a, b, preferred_element_type=F32)


def attend_kernel(
    key_start, query_start, place, *refs, head
):
    q_in = refs[:4]
    shards = refs[4:8]
    out, q_ref, kv_ref, acc, top, fresh, sums, sems = refs[8:]
    copies = []
    for b in range(BLOCKS):
        copies.append((q_in[b // 2].at[b % 2, :, head * GROUP : (head + 1) * GROUP, :], q_ref.at[b]))
    for s, source in enumerate(shards):
        copies.append((source.at[:, SLOTS:KEYS], fresh.at[:, s * SPAN : (s + 1) * SPAN]))
    for s, source in enumerate(shards):
        copies.append((source, kv_ref.at[s]))
    copies = [pltpu.make_async_copy(a, b, sems.at[n]) for n, (a, b) in enumerate(copies)]
    for copy in copies:
        copy.start()
    for copy in copies[:-3]:
        copy.wait()

    lane = lax.broadcasted_iota(jnp.int32, (1, 128), 1)
    slot = lax.broadcasted_iota(jnp.int32, (128, 1), 0)

    def length_of(shard):
        digits = kv_ref[shard, 0, KEYS:PACKED].astype(F32)
        return (jnp.max(digits[0:1]) * 16.0 + jnp.max(digits[1:2])).astype(jnp.int32)

    own_length = length_of(0)
    position = jnp.zeros((1, 128), jnp.int32)
    for s in range(4):
        position = jnp.where(lane // SPAN == s, key_start[s] + lane - s * SPAN, position)

    def queries_of(r):
        first = (r % ROWS) // GROUP
        return q_ref[r // ROWS, first : first + SUB // GROUP].reshape(SUB, 128)

    def limit_of(block, first):
        token = lax.broadcasted_iota(jnp.int32, (SUB, 128), 0) // GROUP
        return token + (query_start[block] + first)

    ones = jnp.ones((128, 128), BF16)
    k_first = jnp.concatenate([fresh[0], kv_ref[0, 0, 0:128]], 0)
    v_first = jnp.concatenate([fresh[1], kv_ref[0, 1, 0:128]], 0)
    v_first = jnp.concatenate([v_first, jnp.concatenate([ones, ones], 0)], 1)
    for r in range(0, BLOCKS * ROWS, SUB):
        scores = times_transposed(queries_of(r), k_first)
        limit = limit_of(r // ROWS, (r % ROWS) // GROUP)
        s0 = jnp.where(position <= limit, scores[:, :128], HIDDEN)
        s1 = jnp.where(lane < own_length, scores[:, 128:], HIDDEN)
        largest = jnp.max(jnp.maximum(s0, s1), axis=1, keepdims=True)
        base = jnp.broadcast_to(largest * SCALE, (SUB, 128))
        top[r : r + SUB] = base
        p0 = jnp.exp2(s0 * SCALE - base).astype(BF16)
        p1 = jnp.exp2(s1 * SCALE - base).astype(BF16)
        acc[r : r + SUB] = times(jnp.concatenate([p0, p1], 1), v_first)

    for copy in copies[-3:]:
        copy.wait()
    lengths = [own_length, *(length_of(s) for s in range(1, 4))]
    begins = [jnp.int32(0)]
    for s in range(4):
        begins.append(begins[-1] + (lengths[s] + 127) // 128)
    count = begins[4]

    def half(index):
        shard, begin, length = jnp.int32(0), jnp.int32(0), lengths[0]
        for s in range(1, 4):
            later = index >= begins[s]
            shard = jnp.where(later, s, shard)
            begin = jnp.where(later, begins[s], begin)
            length = jnp.where(later, lengths[s], length)
        row = (index - begin) * 128
        exists = index < count
        filled = jnp.where(exists, length - row, 0)
        row = jnp.where(exists, row, 0)
        return shard, pl.multiple_of(row, 128), filled

    def step(first, halves):
        parts = [half(first + g) for g in range(halves)]
        k = jnp.concatenate([kv_ref[s, 0, pl.ds(row, 128)] for s, row, _ in parts], 0)
        v = jnp.concatenate(
            [
                jnp.concatenate(
                    [
                        jnp.where(slot < filled, kv_ref[s, 1, pl.ds(row, 128)], 0),
                        jnp.where(slot < filled, ones, 0),
                    ],
                    1,
                )
                for s, row, filled in parts
            ],
            0,
        )
        for r in range(0, BLOCKS * ROWS, SUB):
            scores = times_transposed(queries_of(r), k)
            base = top[r : r + SUB]
            probs = [
                jnp.exp2(scores[:, g * 128 : (g + 1) * 128] * SCALE - base).astype(BF16)
                for g in range(halves)
            ]
            acc[r : r + SUB] += times(jnp.concatenate(probs, 1), v)

    def full_step(number, carry):
        step(HALVES * number + 1, HALVES)
        return carry

    steps = count // HALVES
    lax.fori_loop(0, steps, full_step, 0)
    begun = steps * HALVES + 1
    pairs = (jnp.maximum(count - begun, 0) + 1) // 2

    @pl.when(pairs >= 2)
    def _():
        step(begun, 4)

    @pl.when(pairs % 2 == 1)
    def _():
        step(begun + pairs // 2 * 4, 2)

    diagonal = lax.broadcasted_iota(jnp.int32, (128, 128), 0) == lane

    def in_rows(array, begin):
        rows = []
        for r in range(0, BLOCKS * ROWS, 128):
            square = jnp.where(diagonal, array[r : r + 128, begin : begin + 128], 0.0)
            rows.append(jnp.sum(square, axis=0, keepdims=True))
        return jnp.concatenate(rows, 0)

    sums[...] = in_rows(acc, 128)
    wrong = jnp.where(sums[...] < SUM_LIMIT, 0.0, 1.0)

    @pl.when(jnp.max(wrong) > 0.5)
    def _():
        def redo(tile, carry):
            block, first = tile // 2, (tile % 2) * (SUB // GROUP)
            rows = pl.ds(pl.multiple_of(tile * SUB, SUB), SUB)
            q = q_ref[block, pl.ds(first, SUB // GROUP)].reshape(SUB, 128)

            def absorb(scores, v, state):
                old, total = state
                new = jnp.maximum(old, jnp.max(scores, axis=1, keepdims=True) * SCALE)
                shrink = jnp.exp2(old - new)
                p = jnp.exp2(scores * SCALE - new)
                total = total * shrink + jnp.sum(p, axis=1, keepdims=True)
                acc[rows, 0:128] = acc[rows, 0:128] * shrink + times(p.astype(BF16), v)
                return new, total

            acc[rows] = jnp.zeros((SUB, 256), F32)
            state = (jnp.full((SUB, 1), HIDDEN, F32), jnp.zeros((SUB, 1), F32))

            def more(index, state):
                s, row, filled = half(index)
                scores = times_transposed(q, kv_ref[s, 0, pl.ds(row, 128)])
                scores = jnp.where(lane < filled, scores, HIDDEN)
                return absorb(scores, kv_ref[s, 1, pl.ds(row, 128)], state)

            state = lax.fori_loop(0, count, more, state)
            scores = times_transposed(q, fresh[0])
            scores = jnp.where(position <= limit_of(block, first), scores, HIDDEN)
            base, total = absorb(scores, fresh[1], state)
            top[rows] = jnp.broadcast_to(base, (SUB, 128))
            acc[rows, 128:256] = jnp.broadcast_to(total, (SUB, 128))
            return carry

        lax.fori_loop(0, BLOCKS * ROWS // SUB, redo, 0)
        sums[...] = in_rows(acc, 128)

    notes = []
    for value in (in_rows(top, 0), sums[...]):
        high = value.astype(BF16)
        rest = value - high.astype(F32)
        middle = rest.astype(BF16)
        notes += [high, middle, (rest - middle.astype(F32)).astype(BF16)]
    blank = jnp.zeros((NOTE - 128 - 6, 128), BF16)
    for b in range(BLOCKS):
        for quarter in range(4):
            n = b * 4 + quarter
            out[place[b], quarter, 0:128] = acc[n * 128 : n * 128 + 128, 0:128].astype(BF16)
            rows = [note[n : n + 1] for note in notes]
            out[place[b], quarter, 128:NOTE] = jnp.concatenate([*rows, blank], 0)


def attend(scalars, queries, kv, head):
    return pl.pallas_call(
        functools.partial(attend_kernel, head=head),
        out_shape=jax.ShapeDtypeStruct((BLOCKS, 4, NOTE, 128), BF16),
        in_specs=[pl.BlockSpec(memory_space=pltpu.SMEM)] * 3
        + [pl.BlockSpec(memory_space=pltpu.HBM)] * 8,
        out_specs=pl.BlockSpec(memory_space=pltpu.VMEM),
        scratch_shapes=[
            pltpu.VMEM((BLOCKS, SPAN, GROUP, 128), BF16),
            pltpu.VMEM((4, 2, PACKED, 128), BF16),
            pltpu.VMEM((BLOCKS * ROWS, 256), F32),
            pltpu.VMEM((BLOCKS * ROWS, 128), F32),
            pltpu.VMEM((2, 128, 128), BF16),
            pltpu.VMEM((BLOCKS * 4, 128), F32),
            pltpu.SemaphoreType.DMA((BLOCKS + 8,)),
        ],
        compiler_params=pltpu.CompilerParams(vmem_limit_bytes=62 << 20),
        cost_estimate=pl.CostEstimate(
            flops=2 * 2 * BLOCKS * ROWS * 4 * KEYS * 256,
            bytes_accessed=8 << 20,
            transcendentals=0,
        ),
        name="attend",
    )(*scalars, *queries, *kv)


def merge_kernel(first, second, out):
    eye = lax.broadcasted_iota(jnp.int32, (128, 128), 0) == lax.broadcasted_iota(jnp.int32, (128, 128), 1)
    for source in range(4):
        for head, ref in enumerate((first, second)):
            tops, sums = [], []
            for b in range(BLOCKS):
                note = ref[b * 4 + source, 128:NOTE].astype(F32)
                tops.append(note[0:1] + note[1:2] + note[2:3])
                sums.append(note[3:4] + note[4:5] + note[5:6])
            largest = functools.reduce(jnp.maximum, tops)
            weights = [jnp.exp2(t - largest) for t in tops]
            total = functools.reduce(jnp.add, [w * s for w, s in zip(weights, sums)])
            left, right = [], []
            for b in range(BLOCKS):
                weight = jnp.broadcast_to(weights[b] / total, (128, 128))
                high = weight.astype(BF16)
                low = (weight - high.astype(F32)).astype(BF16)
                left += [jnp.where(eye, high, 0), jnp.where(eye, low, 0)]
                partial = ref[b * 4 + source, 0:128]
                right += [partial, partial]
            merged = times(jnp.concatenate(left, 1), jnp.concatenate(right, 0))
            begin = source * 32 + head * GROUP
            out[:, begin : begin + GROUP] = merged.astype(BF16).reshape(8, GROUP, 128)


def merge(first, second):
    return pl.pallas_call(
        merge_kernel,
        out_shape=jax.ShapeDtypeStruct((8, 128, 128), BF16),
        in_specs=[pl.BlockSpec(memory_space=pltpu.VMEM)] * 2,
        out_specs=pl.BlockSpec(memory_space=pltpu.VMEM),
        compiler_params=pltpu.CompilerParams(vmem_limit_bytes=32 << 20),
        name="merge",
    )(first, second)


def moved(block, axis, distance):
    size = lax.axis_size(axis)
    return lax.ppermute(block, axis, [(i, (i + distance) % size) for i in range(size)])


def per_device(queries, cache_keys, cache_values, new_keys, new_values, lengths, span_offset):
    x, z, y = lax.axis_index("x"), lax.axis_index("z"), lax.axis_index("y")

    digit = lax.broadcasted_iota(jnp.int32, (16, 128), 0)
    length = lengths[0]
    tail = jnp.where(digit == 0, length // 16, jnp.where(digit == 1, length % 16, 0)).astype(BF16)

    def packed(head):
        k = jnp.concatenate([cache_keys[:, head], new_keys[:, head], tail], 0)
        v = jnp.concatenate([cache_values[:, head], new_values[:, head], tail], 0)
        return jnp.stack([k, v])

    beside = moved(queries, "z", 1)
    queries, beside, own = lax.optimization_barrier((queries, beside, packed(0)))
    left, right, far = (moved(own, "y", distance) for distance in (1, -1, 2))
    both = jnp.stack([queries, beside])
    after, before = moved(both, "x", -1), moved(both, "x", 1)
    both_too, after, before = lax.optimization_barrier((both, after, before))
    blocks = (both, after, before, moved(both_too, "x", 2))
    left, right, far, late_own = lax.optimization_barrier((left, right, far, packed(1)))
    early = (own, left, right, far)
    late = (late_own, *(moved(late_own, "y", distance) for distance in (1, -1, 2)))
    kv = (early, late)
    homes = [((x + dx) % 4, (z + dz) % 2) for dx in (0, 1, -1, 2) for dz in (0, 1)]
    place = jnp.stack([hx * 2 + hz for hx, hz in homes]).astype(jnp.int32)
    query_start = jnp.stack([(hx * 8 + hz * 4 + y) * SPAN for hx, hz in homes]).astype(jnp.int32) + span_offset
    shards = jnp.stack([y, (y - 1) % 4, (y + 1) % 4, (y + 2) % 4]).astype(jnp.int32)
    key_start = (x * 8 + z * 4 + shards) * SPAN
    scalars = (key_start, query_start, place)

    partials = []
    for head in range(2):
        partial = attend(scalars, blocks, kv[head], head)
        partials.append(
            lax.all_to_all(
                partial.reshape(BLOCKS * 4, NOTE, 128), ("x", "z", "head"), 0, 0, tiled=True
            )
        )
    return merge(*partials)


def solution(mesh):
    inner = Mesh(mesh.devices.reshape(4, 2, 4, 4), ("x", "z", "y", "head"))
    context = ("x", "z", "y")
    return jax.shard_map(
        per_device,
        mesh=inner,
        in_specs=(
            P(context, "head", None),
            P(context, "head", None),
            P(context, "head", None),
            P(context, "head", None),
            P(context, "head", None),
            P(context),
            P(),
        ),
        out_specs=P((*context, "head"), None, None),
        check_vma=False,
    )
```

```python
import functools
import math

import jax
import jax.numpy as jnp
from jax import lax
from jax.experimental import pallas as pl
from jax.experimental.pallas import tpu as pltpu
from jax.sharding import Mesh, PartitionSpec as P

F32 = jnp.float32
BF16 = jnp.bfloat16
SCALE = math.log2(math.e) / math.sqrt(128)
HIDDEN = -1e30
SUM_LIMIT = 1e30
SLOTS = 1280
SPAN = 32
KEYS = SLOTS + SPAN
PACKED = KEYS + 16
GROUP = 16
ROWS = SPAN * GROUP
BLOCKS = 8
SUB = 256
NOTE = 144
HALVES = 8


def times_transposed(a, b):
    return lax.dot_general(a, b, (((1,), (1,)), ((), ())), preferred_element_type=F32)


def times(a, b):
    return jnp.dot(a, b, preferred_element_type=F32)


def attend_kernel(
    key_start, query_start, place, *refs, head
):
    q_in = refs[:4]
    shards = refs[4:8]
    out, q_ref, kv_ref, acc, top, fresh, sums, sems = refs[8:]
    copies = []
    for b in range(BLOCKS):
        copies.append((q_in[b // 2].at[b % 2, :, head * GROUP : (head + 1) * GROUP, :], q_ref.at[b]))
    for s, source in enumerate(shards):
        copies.append((source.at[:, SLOTS:KEYS], fresh.at[:, s * SPAN : (s + 1) * SPAN]))
    for s, source in enumerate(shards):
        copies.append((source, kv_ref.at[s]))
    copies = [pltpu.make_async_copy(a, b, sems.at[n]) for n, (a, b) in enumerate(copies)]
    for copy in copies:
        copy.start()
    for copy in copies[:-3]:
        copy.wait()

    lane = lax.broadcasted_iota(jnp.int32, (1, 128), 1)
    slot = lax.broadcasted_iota(jnp.int32, (128, 1), 0)

    def length_of(shard):
        digits = kv_ref[shard, 0, KEYS:PACKED].astype(F32)
        return (jnp.max(digits[0:1]) * 16.0 + jnp.max(digits[1:2])).astype(jnp.int32)

    own_length = length_of(0)
    position = jnp.zeros((1, 128), jnp.int32)
    for s in range(4):
        position = jnp.where(lane // SPAN == s, key_start[s] + lane - s * SPAN, position)

    def queries_of(r):
        first = (r % ROWS) // GROUP
        return q_ref[r // ROWS, first : first + SUB // GROUP].reshape(SUB, 128)

    def limit_of(block, first):
        token = lax.broadcasted_iota(jnp.int32, (SUB, 128), 0) // GROUP
        return token + (query_start[block] + first)

    ones = jnp.ones((128, 128), BF16)
    k_first = jnp.concatenate([fresh[0], kv_ref[0, 0, 0:128]], 0)
    v_first = jnp.concatenate([fresh[1], kv_ref[0, 1, 0:128]], 0)
    v_first = jnp.concatenate([v_first, jnp.concatenate([ones, ones], 0)], 1)
    for r in range(0, BLOCKS * ROWS, SUB):
        scores = times_transposed(queries_of(r), k_first)
        limit = limit_of(r // ROWS, (r % ROWS) // GROUP)
        s0 = jnp.where(position <= limit, scores[:, :128], HIDDEN)
        s1 = jnp.where(lane < own_length, scores[:, 128:], HIDDEN)
        largest = jnp.max(jnp.maximum(s0, s1), axis=1, keepdims=True)
        base = jnp.broadcast_to(largest * SCALE, (SUB, 128))
        top[r : r + SUB] = base
        p0 = jnp.exp2(s0 * SCALE - base).astype(BF16)
        p1 = jnp.exp2(s1 * SCALE - base).astype(BF16)
        acc[r : r + SUB] = times(jnp.concatenate([p0, p1], 1), v_first)

    for copy in copies[-3:]:
        copy.wait()
    lengths = [own_length, *(length_of(s) for s in range(1, 4))]
    begins = [jnp.int32(0)]
    for s in range(4):
        begins.append(begins[-1] + (lengths[s] + 127) // 128)
    count = begins[4]

    def half(index):
        shard, begin, length = jnp.int32(0), jnp.int32(0), lengths[0]
        for s in range(1, 4):
            later = index >= begins[s]
            shard = jnp.where(later, s, shard)
            begin = jnp.where(later, begins[s], begin)
            length = jnp.where(later, lengths[s], length)
        row = (index - begin) * 128
        exists = index < count
        filled = jnp.where(exists, length - row, 0)
        row = jnp.where(exists, row, 0)
        return shard, pl.multiple_of(row, 128), filled

    def step(first, halves):
        parts = [half(first + g) for g in range(halves)]
        k = jnp.concatenate([kv_ref[s, 0, pl.ds(row, 128)] for s, row, _ in parts], 0)
        v = jnp.concatenate(
            [
                jnp.concatenate(
                    [
                        jnp.where(slot < filled, kv_ref[s, 1, pl.ds(row, 128)], 0),
                        jnp.where(slot < filled, ones, 0),
                    ],
                    1,
                )
                for s, row, filled in parts
            ],
            0,
        )
        for r in range(0, BLOCKS * ROWS, SUB):
            scores = times_transposed(queries_of(r), k)
            base = top[r : r + SUB]
            probs = [
                jnp.exp2(scores[:, g * 128 : (g + 1) * 128] * SCALE - base).astype(BF16)
                for g in range(halves)
            ]
            acc[r : r + SUB] += times(jnp.concatenate(probs, 1), v)

    def full_step(number, carry):
        step(HALVES * number + 1, HALVES)
        return carry

    steps = count // HALVES
    lax.fori_loop(0, steps, full_step, 0)
    begun = steps * HALVES + 1
    pairs = (jnp.maximum(count - begun, 0) + 1) // 2

    @pl.when(pairs >= 2)
    def _():
        step(begun, 4)

    @pl.when(pairs % 2 == 1)
    def _():
        step(begun + pairs // 2 * 4, 2)

    diagonal = lax.broadcasted_iota(jnp.int32, (128, 128), 0) == lane

    def in_rows(array, begin):
        rows = []
        for r in range(0, BLOCKS * ROWS, 128):
            square = jnp.where(diagonal, array[r : r + 128, begin : begin + 128], 0.0)
            rows.append(jnp.sum(square, axis=0, keepdims=True))
        return jnp.concatenate(rows, 0)

    sums[...] = in_rows(acc, 128)
    wrong = jnp.where(sums[...] < SUM_LIMIT, 0.0, 1.0)

    @pl.when(jnp.max(wrong) > 0.5)
    def _():
        def redo(tile, carry):
            block, first = tile // 2, (tile % 2) * (SUB // GROUP)
            rows = pl.ds(pl.multiple_of(tile * SUB, SUB), SUB)
            q = q_ref[block, pl.ds(first, SUB // GROUP)].reshape(SUB, 128)

            def absorb(scores, v, state):
                old, total = state
                new = jnp.maximum(old, jnp.max(scores, axis=1, keepdims=True) * SCALE)
                shrink = jnp.exp2(old - new)
                p = jnp.exp2(scores * SCALE - new)
                total = total * shrink + jnp.sum(p, axis=1, keepdims=True)
                acc[rows, 0:128] = acc[rows, 0:128] * shrink + times(p.astype(BF16), v)
                return new, total

            acc[rows] = jnp.zeros((SUB, 256), F32)
            state = (jnp.full((SUB, 1), HIDDEN, F32), jnp.zeros((SUB, 1), F32))

            def more(index, state):
                s, row, filled = half(index)
                scores = times_transposed(q, kv_ref[s, 0, pl.ds(row, 128)])
                scores = jnp.where(lane < filled, scores, HIDDEN)
                return absorb(scores, kv_ref[s, 1, pl.ds(row, 128)], state)

            state = lax.fori_loop(0, count, more, state)
            scores = times_transposed(q, fresh[0])
            scores = jnp.where(position <= limit_of(block, first), scores, HIDDEN)
            base, total = absorb(scores, fresh[1], state)
            top[rows] = jnp.broadcast_to(base, (SUB, 128))
            acc[rows, 128:256] = jnp.broadcast_to(total, (SUB, 128))
            return carry

        lax.fori_loop(0, BLOCKS * ROWS // SUB, redo, 0)
        sums[...] = in_rows(acc, 128)

    notes = []
    for value in (in_rows(top, 0), sums[...]):
        high = value.astype(BF16)
        rest = value - high.astype(F32)
        middle = rest.astype(BF16)
        notes += [high, middle, (rest - middle.astype(F32)).astype(BF16)]
    blank = jnp.zeros((NOTE - 128 - 6, 128), BF16)
    for b in range(BLOCKS):
        for quarter in range(4):
            n = b * 4 + quarter
            out[place[b], quarter, 0:128] = acc[n * 128 : n * 128 + 128, 0:128].astype(BF16)
            rows = [note[n : n + 1] for note in notes]
            out[place[b], quarter, 128:NOTE] = jnp.concatenate([*rows, blank], 0)


def attend(scalars, queries, kv, head):
    return pl.pallas_call(
        functools.partial(attend_kernel, head=head),
        out_shape=jax.ShapeDtypeStruct((BLOCKS, 4, NOTE, 128), BF16),
        in_specs=[pl.BlockSpec(memory_space=pltpu.SMEM)] * 3
        + [pl.BlockSpec(memory_space=pltpu.HBM)] * 8,
        out_specs=pl.BlockSpec(memory_space=pltpu.VMEM),
        scratch_shapes=[
            pltpu.VMEM((BLOCKS, SPAN, GROUP, 128), BF16),
            pltpu.VMEM((4, 2, PACKED, 128), BF16),
            pltpu.VMEM((BLOCKS * ROWS, 256), F32),
            pltpu.VMEM((BLOCKS * ROWS, 128), F32),
            pltpu.VMEM((2, 128, 128), BF16),
            pltpu.VMEM((BLOCKS * 4, 128), F32),
            pltpu.SemaphoreType.DMA((BLOCKS + 8,)),
        ],
        compiler_params=pltpu.CompilerParams(vmem_limit_bytes=62 << 20),
        cost_estimate=pl.CostEstimate(
            flops=2 * 2 * BLOCKS * ROWS * 4 * KEYS * 256,
            bytes_accessed=8 << 20,
            transcendentals=0,
        ),
        name="attend",
    )(*scalars, *queries, *kv)


def merge_kernel(first, second, out):
    eye = lax.broadcasted_iota(jnp.int32, (128, 128), 0) == lax.broadcasted_iota(jnp.int32, (128, 128), 1)
    for source in range(4):
        for head, ref in enumerate((first, second)):
            tops, sums = [], []
            for b in range(BLOCKS):
                note = ref[b * 4 + source, 128:NOTE].astype(F32)
                tops.append(note[0:1] + note[1:2] + note[2:3])
                sums.append(note[3:4] + note[4:5] + note[5:6])
            largest = functools.reduce(jnp.maximum, tops)
            weights = [jnp.exp2(t - largest) for t in tops]
            total = functools.reduce(jnp.add, [w * s for w, s in zip(weights, sums)])
            left, right = [], []
            for b in range(BLOCKS):
                weight = jnp.broadcast_to(weights[b] / total, (128, 128))
                high = weight.astype(BF16)
                low = (weight - high.astype(F32)).astype(BF16)
                left += [jnp.where(eye, high, 0), jnp.where(eye, low, 0)]
                partial = ref[b * 4 + source, 0:128]
                right += [partial, partial]
            merged = times(jnp.concatenate(left, 1), jnp.concatenate(right, 0))
            begin = source * 32 + head * GROUP
            out[:, begin : begin + GROUP] = merged.astype(BF16).reshape(8, GROUP, 128)


def merge(first, second):
    return pl.pallas_call(
        merge_kernel,
        out_shape=jax.ShapeDtypeStruct((8, 128, 128), BF16),
        in_specs=[pl.BlockSpec(memory_space=pltpu.VMEM)] * 2,
        out_specs=pl.BlockSpec(memory_space=pltpu.VMEM),
        compiler_params=pltpu.CompilerParams(vmem_limit_bytes=32 << 20),
        name="merge",
    )(first, second)


def moved(block, axis, distance):
    size = lax.axis_size(axis)
    return lax.ppermute(block, axis, [(i, (i + distance) % size) for i in range(size)])


def per_device(queries, cache_keys, cache_values, new_keys, new_values, lengths, span_offset):
    x, z, y = lax.axis_index("x"), lax.axis_index("z"), lax.axis_index("y")

    digit = lax.broadcasted_iota(jnp.int32, (16, 128), 0)
    length = lengths[0]
    tail = jnp.where(digit == 0, length // 16, jnp.where(digit == 1, length % 16, 0)).astype(BF16)

    def packed(head):
        k = jnp.concatenate([cache_keys[:, head], new_keys[:, head], tail], 0)
        v = jnp.concatenate([cache_values[:, head], new_values[:, head], tail], 0)
        return jnp.stack([k, v])

    beside = moved(queries, "z", 1)
    queries, beside, own = lax.optimization_barrier((queries, beside, packed(0)))
    left, right, far = (moved(own, "y", distance) for distance in (1, -1, 2))
    both = jnp.stack([queries, beside])
    after, before = moved(both, "x", -1), moved(both, "x", 1)
    both_too, after, before = lax.optimization_barrier((both, after, before))
    blocks = (both, after, before, moved(both_too, "x", 2))
    left, right, late_own = lax.optimization_barrier((left, right, packed(1)))
    early = (own, left, right, far)
    late = (late_own, *(moved(late_own, "y", distance) for distance in (1, -1, 2)))
    kv = (early, late)
    homes = [((x + dx) % 4, (z + dz) % 2) for dx in (0, 1, -1, 2) for dz in (0, 1)]
    place = jnp.stack([hx * 2 + hz for hx, hz in homes]).astype(jnp.int32)
    query_start = jnp.stack([(hx * 8 + hz * 4 + y) * SPAN for hx, hz in homes]).astype(jnp.int32) + span_offset
    shards = jnp.stack([y, (y - 1) % 4, (y + 1) % 4, (y + 2) % 4]).astype(jnp.int32)
    key_start = (x * 8 + z * 4 + shards) * SPAN
    scalars = (key_start, query_start, place)

    partials = []
    for head in range(2):
        partial = attend(scalars, blocks, kv[head], head)
        partials.append(
            lax.all_to_all(
                partial.reshape(BLOCKS * 4, NOTE, 128), ("x", "z", "head"), 0, 0, tiled=True
            )
        )
    return merge(*partials)


def solution(mesh):
    inner = Mesh(mesh.devices.reshape(4, 2, 4, 4), ("x", "z", "y", "head"))
    context = ("x", "z", "y")
    return jax.shard_map(
        per_device,
        mesh=inner,
        in_specs=(
            P(context, "head", None),
            P(context, "head", None),
            P(context, "head", None),
            P(context, "head", None),
            P(context, "head", None),
            P(context),
            P(),
        ),
        out_specs=P((*context, "head"), None, None),
        check_vma=False,
    )
```
